32 devices in a mesh: grp: 4 (over z), dev: 8 (over y, x, core).
Axes of the slice: x: 2, y: 2, z: 4, core: 2. Of those that a mesh axis runs over, the one named last changes fastest.
Arguments:
- stiff_rows: bfloat16 [32, 6, 384, 384], P(('grp', 'dev')), may hold values from -0.75 to 0.75
- stiff_iface: bfloat16 [32, 2, 384, 384], P(('grp', 'dev')), may hold values from -0.75 to 0.75
- columns: int32 [32, 6], P(('grp', 'dev')), may hold values from 0 to 7, as said below
- live_count: int32 [32], P(('grp', 'dev')), may hold values from 2 to 6
- aggregate: int32 [32], P(('grp', 'dev')), may hold values from 0 to 1
- prolong: bfloat16 [32, 384, 384], P(('grp', 'dev')), may hold values from -0.3125 to 0.3125
Outputs:
- coarse_band: float32 [3072, 2304], P(('grp', 'dev'))
The draws below stay inside these ranges and needn't reach their ends.
Inputs may be any that keep to these rules, and one draw needn't show every extreme that they name: The 6 columns of a row are distinct, the first is the row's own position p, and each lies within 3 positions of p around the cycle of 8 positions of the slab.
All inputs are finite; a program needn't handle non-finite values.
Results may differ from the reference program's by a relative error of at most 0.018.
Values may be sent and summed in bfloat16 or wider, within the bound.
No kernel may reach another device: no remote copies, remote signals or barrier semaphores. Data moves between devices by JAX's collectives and lax.ppermute only.
A program may use at most 64 MiB of HBM per device.

```python
import jax
import jax.numpy as jnp
from jax import lax

NB = 384
SLOTS = 6
REACH = 3
COARSE = 2
FINE = 32
CROWS = 3072
N_GRP = 4
N_DEV = 8


def draw_columns(key, part):
    offsets = jnp.concatenate([jnp.arange(-REACH, 0, dtype=jnp.int32), jnp.arange(1, REACH + 1, dtype=jnp.int32)])
    row_keys = jax.random.split(key, FINE)
    orders = jax.vmap(lambda k: jax.random.permutation(k, 2 * REACH))(row_keys)
    chosen = offsets[orders[:, :SLOTS - 1]]
    shifts = jnp.concatenate([jnp.zeros((FINE, 1), jnp.int32), chosen], axis=1)
    position = (jnp.arange(FINE, dtype=jnp.int32) % N_DEV)[:, None]
    return ((position + shifts + N_DEV) % N_DEV).astype(jnp.int32)


def touch_ends(entries, rng, least, top_value):
    extent = entries.shape
    spot = [jax.random.randint(jax.random.fold_in(rng, axis), (), 0, extent[axis]) for axis in range(len(extent))]
    entries = entries.at[tuple(spot)].set(least)
    longest = extent.index(max(extent))
    spot[longest] = (spot[longest] + 1) % extent[longest]
    return entries.at[tuple(spot)].set(top_value)


def block_levels(key, extent, pieces, low, largest):
    level, own = 1.0, jax.random.fold_in(key, 6)
    for axis_at, parts in pieces:
        draws = jnp.exp(jax.random.uniform(jax.random.fold_in(own, axis_at), (parts,), jnp.float32, low / len(pieces), largest / len(pieces)))
        level = level * jnp.repeat(draws, extent[axis_at] // parts).reshape([-1 if axis == axis_at else 1 for axis in range(len(extent))])
    return level


def gaussian(own_key, shape, scale, limit, cuts=(), kind=jnp.bfloat16):
    values = scale * jax.random.normal(own_key, shape, jnp.float32)
    if cuts:
        values = values * block_levels(own_key, shape, cuts, -0.22, 0.18)
    return jnp.clip(values, -limit, limit).astype(kind)


def setup_inputs(seed: int = 0) -> dict:
    keys = jax.random.split(jax.random.key(seed), 7)
    return {
        "stiff_rows": gaussian(keys[0], (FINE, SLOTS, NB, NB), 0.125, 0.75, ((0, 32),)),
        "stiff_iface": gaussian(keys[1], (FINE, 2, NB, NB), 0.125, 0.75, ((0, 32),)),
        "columns": draw_columns(jax.random.fold_in(keys[6], 71), 0),
        "live_count": touch_ends(jax.random.randint(keys[3], (FINE,), 2, SLOTS + 1), jax.random.fold_in(keys[3], 1), 2, SLOTS).astype(jnp.int32),
        "aggregate": touch_ends(jax.random.randint(keys[4], (FINE,), 0, COARSE), jax.random.fold_in(keys[4], 1), 0, COARSE - 1).astype(jnp.int32),
        "prolong": gaussian(keys[5], (FINE, NB, NB), NB ** -0.5, 0.3125, ((0, 32),)),
    }


def reference(stiff_rows, stiff_iface, columns, live_count, aggregate, prolong):
    width = 3 * COARSE * NB
    start_band = jnp.zeros((CROWS, width), jnp.float32)
    sides = jnp.concatenate([jnp.ones((SLOTS,), jnp.int32), jnp.array([0, 2], jnp.int32)])

    def one_row(band, index):
        group_at = index // N_DEV
        coupled = (group_at * N_DEV + columns[index]).astype(jnp.int32)
        lower_row = jnp.maximum(index - N_DEV, 0).astype(jnp.int32)
        upper_row = jnp.minimum(index + N_DEV, FINE - 1).astype(jnp.int32)
        blocks = jnp.concatenate([prolong[coupled], prolong[lower_row][None], prolong[upper_row][None]], axis=0)
        stiff = jnp.concatenate([stiff_rows[index], stiff_iface[index]], axis=0)
        qmat = jnp.einsum("kfg,kgm->kfm", stiff.astype(jnp.float32), blocks.astype(jnp.float32)).astype(jnp.bfloat16)
        contrib = jnp.einsum("fc,kfm->kcm", prolong[index].astype(jnp.float32), qmat.astype(jnp.float32))
        targets = jnp.concatenate([aggregate[coupled], aggregate[lower_row][None], aggregate[upper_row][None]])
        weights = jnp.concatenate([
            (jnp.arange(SLOTS, dtype=jnp.int32) < live_count[index]).astype(jnp.float32),
            (group_at > 0).astype(jnp.float32)[None],
            (group_at < N_GRP - 1).astype(jnp.float32)[None]])
        side_hot = (sides[:, None] == jnp.arange(3, dtype=jnp.int32)[None, :]).astype(jnp.float32)
        block_hot = (targets[:, None] == jnp.arange(COARSE, dtype=jnp.int32)[None, :]).astype(jnp.float32)
        placing = side_hot[:, :, None] * block_hot[:, None, :] * weights[:, None, None]
        partial_value = jnp.einsum("ksb,kcm->csbm", placing, contrib).reshape(NB, width)
        partial_value = lax.optimization_barrier(partial_value.astype(jnp.bfloat16)).astype(jnp.float32)
        row_start = ((group_at * COARSE + aggregate[index]) * NB).astype(jnp.int32)
        zero_col = jnp.zeros((), jnp.int32)
        current = lax.dynamic_slice(band, (row_start, zero_col), (NB, width))
        band = lax.dynamic_update_slice(band, current + partial_value, (row_start, zero_col))
        return band, None

    band, _ = lax.scan(one_row, start_band, jnp.arange(FINE, dtype=jnp.int32))
    return band
```

```python
import jax
import jax.numpy as jnp
from jax import lax
from jax.experimental import pallas as pl
from jax.experimental.pallas import tpu as pltpu
from jax.sharding import PartitionSpec as P

NB = 384
SLOTS = 6
REACH = 3
COARSE = 2
QUARTER = NB // 4
META = 16
LANES = (0, 1, 2, 3, 5, 6, 7)
F32 = jnp.float32
BF16 = jnp.bfloat16


def passed_along(block, axis, distance):
    devices = range(lax.axis_size(axis))
    route = [((i - distance) % len(devices), i) for i in devices]
    return lax.ppermute(block, axis, route)


def extended(array, sides, width):
    for axis, dim in sides:
        count, length = (lax.axis_size(axis), array.shape[dim])
        up = [(i, (i + 1) % count) for i in range(count - 1)]
        down = [(j, i) for i, j in up]
        last = lax.slice_in_dim(array, length - width, length, axis=dim)
        initial = lax.slice_in_dim(array, 0, width, axis=dim)
        before = lax.ppermute(last, axis, up)
        after = lax.ppermute(initial, axis, down)
        array = jnp.concatenate([before, array, after], axis=dim)
    return array


def on_any_slab(stiff_rows, stiff_iface, columns, live_count, aggregate, prolong):
    dev_count = lax.axis_size("dev")
    grp_count = lax.axis_size("grp")
    group_at = lax.axis_index("grp")
    place_at = lax.axis_index("dev")
    my_columns = columns[0]
    block_list = []
    agg_list = []
    for offset in range(-REACH, REACH + 1):
        if offset == 0:
            block_list.append(prolong)
            agg_list.append(aggregate)
        else:
            got = passed_along((prolong, aggregate), "dev", -offset)
            block_list.append(got[0])
            agg_list.append(got[1])
    window_blocks = jnp.concatenate(block_list, axis=0)
    window_aggs = jnp.concatenate(agg_list, axis=0)
    offsets = (my_columns - place_at + dev_count + REACH) % dev_count
    panels = jnp.take(window_blocks, offsets, axis=0)
    column_aggs = jnp.take(window_aggs, offsets, axis=0)
    slab_blocks, slab_aggs = (
        extended(prolong, (("grp", 0),), 1),
        extended(aggregate, (("grp", 0),), 1),
    )
    blocks = jnp.concatenate([panels, slab_blocks[0:1], slab_blocks[2:3]], axis=0)
    stiff = jnp.concatenate([stiff_rows[0], stiff_iface[0]], axis=0)
    qmat = jnp.einsum("kfg,kgm->kfm", stiff, blocks, preferred_element_type=F32).astype(BF16)
    contrib = jnp.einsum("fc,kfm->kcm", prolong[0], qmat, preferred_element_type=F32)
    targets = jnp.concatenate([column_aggs, slab_aggs[0][None], slab_aggs[2][None]])
    weights = jnp.concatenate(
        [
            (jnp.arange(SLOTS, dtype=jnp.int32) < live_count[0]).astype(F32),
            (group_at > 0).astype(F32)[None],
            (group_at < grp_count - 1).astype(F32)[None],
        ]
    )
    sides = jnp.concatenate([jnp.ones((SLOTS,), jnp.int32), jnp.array([0, 2], jnp.int32)])
    side_hot = (sides[:, None] == jnp.arange(3, dtype=jnp.int32)[None, :]).astype(F32)
    block_hot = (targets[:, None] == jnp.arange(COARSE, dtype=jnp.int32)[None, :]).astype(F32)
    placing = side_hot[:, :, None] * block_hot[:, None, :] * weights[:, None, None]
    partial_value = jnp.einsum("ksb,kcm->csbm", placing, contrib).reshape(NB, 3 * COARSE * NB)
    partial_value = partial_value.astype(BF16).astype(F32)
    own_hot = (jnp.arange(COARSE, dtype=jnp.int32) == aggregate[0]).astype(F32)
    spread = (own_hot[:, None, None] * partial_value[None]).reshape(COARSE * NB, 3 * COARSE * NB)
    return lax.psum_scatter(
        spread.astype(BF16), "dev", scatter_dimension=0, tiled=True
    ).astype(F32)


def dot(a, b):
    return jnp.dot(a, b, preferred_element_type=F32)


def left_kernel(columns, live, prolong, rows, iface, left, left_iface):
    place = lax.axis_index("dev")
    turned = prolong[0].T
    for s in range(2):
        left_iface[s] = dot(turned, iface[0, s]).astype(BF16)
    for k in range(SLOTS):

        @pl.when(k < live[0])
        def _():
            left[columns[0, k] ^ place] = dot(turned, rows[0, k]).astype(BF16)


def iface_kernel(left_iface, below, above, out0, out1, out2, out3, held):
    quarter = lax.axis_index("dev") % 4
    for s, block in enumerate((below, above)):
        held[s] = dot(left_iface[s], block[:NB]).astype(BF16)
    for t, out in enumerate((out0, out1, out2, out3)):
        start = pl.multiple_of((quarter ^ t) * QUARTER, QUARTER)
        for s, block in enumerate((below, above)):
            out[s * QUARTER : (s + 1) * QUARTER] = held[s, pl.ds(start, QUARTER)]
            out[2 * QUARTER + s * META : 2 * QUARTER + (s + 1) * META] = block[NB:]


def slab_kernel(columns, live, left, b0, b1, b2, b3, b5, b6, b7, out0, out1, out2, out3, held):
    place = lax.axis_index("dev")
    quarter = place % 4
    held[...] = jnp.zeros_like(held)
    for t, block in zip(LANES, (b0, b1, b2, b3, b5, b6, b7)):
        present = jnp.bool_(False)
        for k in range(SLOTS):
            present = present | ((k < live[0]) & ((columns[0, k] ^ place) == t))

        @pl.when(present)
        def _():
            value = dot(left[t], block[:NB])
            upper = block[NB : NB + 1].astype(F32)
            held[0] += value * (1.0 - upper)
            held[1] += value * upper

    for t, out in enumerate((out0, out1, out2, out3)):
        start = pl.multiple_of((quarter ^ t) * QUARTER, QUARTER)
        for b in range(COARSE):
            out[b * QUARTER : (b + 1) * QUARTER] = held[b, pl.ds(start, QUARTER)].astype(BF16)


def summed(own, other, parts, marks, shape_of, kept, sent):
    for column, pieces in enumerate(shape_of(parts)):
        keep, send = None, None
        for value, mark in zip(pieces, marks):
            here = value * (own * mark + other * (1.0 - mark))
            there = value * (other * mark + own * (1.0 - mark))
            keep = here if keep is None else keep + here
            send = there if send is None else send + there
        kept[:, column * NB : (column + 1) * NB] = keep
        sent[:, column * NB : (column + 1) * NB] = send.astype(BF16)


def own_side():
    upper = (lax.axis_index("dev") // 4).astype(F32)
    return upper, 1.0 - upper


def iface_sum_kernel(v0, v1, v2, v3, m0, m1, m2, m3, kept, sent):
    own, other = own_side()

    def shape_of(parts):
        for s in range(2):
            for b in range(COARSE):
                pieces = []
                for v in parts:
                    mark = v[2 * QUARTER + s * META : 2 * QUARTER + s * META + 1].astype(F32)
                    weight = mark if b else 1.0 - mark
                    pieces.append(v[s * QUARTER : (s + 1) * QUARTER].astype(F32) * weight)
                yield pieces

    marks = [m[0:1].astype(F32) for m in (m0, m1, m2, m3)]
    summed(own, other, (v0, v1, v2, v3), marks, shape_of, kept, sent)


def slab_sum_kernel(v0, v1, v2, v3, m0, m1, m2, m3, kept, sent):
    own, other = own_side()

    def shape_of(parts):
        for b in range(COARSE):
            yield [v[b * QUARTER : (b + 1) * QUARTER].astype(F32) for v in parts]

    marks = [m[0:1].astype(F32) for m in (m0, m1, m2, m3)]
    summed(own, other, (v0, v1, v2, v3), marks, shape_of, kept, sent)


def last_kernel(kept_iface, got_iface, kept_slab, got_slab, out):
    wide = COARSE * NB
    out[:, :wide] = kept_iface[:, :wide] + got_iface[:, :wide].astype(F32)
    out[:, wide : 2 * wide] = kept_slab[...] + got_slab[...].astype(F32)
    out[:, 2 * wide :] = kept_iface[:, wide:] + got_iface[:, wide:].astype(F32)


def whole():
    return pl.BlockSpec(memory_space=pltpu.VMEM)


def scalars():
    return pl.BlockSpec(memory_space=pltpu.SMEM)


def mark_rows():
    return pl.BlockSpec((META, NB), lambda i: (NB // META, 0))


def cost(dots, size):
    return pl.CostEstimate(flops=2 * dots * NB**3, bytes_accessed=size, transcendentals=0)


def on_square(stiff_rows, stiff_iface, columns, live_count, aggregate, prolong):
    groups = lax.axis_size("grp")
    up = [(i, i + 1) for i in range(groups - 1)]
    down = [(j, i) for i, j in up]

    def hop(block, turn):
        return lax.ppermute(block, "dev", [(i, i ^ turn) for i in range(8)])

    tail = jnp.broadcast_to(aggregate[0].astype(BF16), (META, NB))
    mine = jnp.concatenate([prolong[0], tail], axis=0)
    below = lax.ppermute(mine, "grp", up)
    above = lax.ppermute(mine, "grp", down)
    b6 = hop(mine, 6)
    b2 = hop(mine, 2)
    b5 = hop(mine, 5)
    b1 = hop(mine, 1)
    b3 = hop(b2, 1)
    b7 = hop(b6, 1)

    left, left_iface = pl.pallas_call(
        left_kernel,
        out_shape=(
            jax.ShapeDtypeStruct((8, NB, NB), BF16),
            jax.ShapeDtypeStruct((2, NB, NB), BF16),
        ),
        in_specs=[scalars(), scalars(), whole(), whole(), whole()],
        out_specs=(whole(), whole()),
        cost_estimate=cost(8, 20 * NB * NB),
        name="left",
    )(columns, live_count, prolong, stiff_rows, stiff_iface)

    part = jax.ShapeDtypeStruct((2 * QUARTER + 2 * META, NB), BF16)
    ti = pl.pallas_call(
        iface_kernel,
        out_shape=(part,) * 4,
        in_specs=[whole()] * 3,
        out_specs=(whole(),) * 4,
        scratch_shapes=[pltpu.VMEM((2, NB, NB), BF16)],
        cost_estimate=cost(2, 8 * NB * NB),
        name="iface",
    )(left_iface, below, above)
    ri = [ti[0]] + [hop(ti[t], t) for t in (1, 2, 3)]

    part = jax.ShapeDtypeStruct((2 * QUARTER, NB), BF16)
    ts = pl.pallas_call(
        slab_kernel,
        out_shape=(part,) * 4,
        in_specs=[scalars(), scalars()] + [whole()] * 8,
        out_specs=(whole(),) * 4,
        scratch_shapes=[pltpu.VMEM((COARSE, NB, NB), F32)],
        cost_estimate=cost(6, 16 * NB * NB),
        name="slab",
    )(columns, live_count, left, mine, b1, b2, b3, b5, b6, b7)
    rs = [ts[0]] + [hop(ts[t], t) for t in (1, 2, 3)]

    marks = (mine, b1, b2, b3)
    kept_iface, sent_iface = pl.pallas_call(
        iface_sum_kernel,
        out_shape=(
            jax.ShapeDtypeStruct((QUARTER, 4 * NB), F32),
            jax.ShapeDtypeStruct((QUARTER, 4 * NB), BF16),
        ),
        grid=(1,),
        in_specs=[whole()] * 4 + [mark_rows()] * 4,
        out_specs=(whole(), whole()),
        cost_estimate=cost(0, 8 * NB * NB),
        name="iface_sum",
    )(*ri, *marks)
    got_iface = hop(sent_iface, 4)
    kept_slab, sent_slab = pl.pallas_call(
        slab_sum_kernel,
        out_shape=(
            jax.ShapeDtypeStruct((QUARTER, 2 * NB), F32),
            jax.ShapeDtypeStruct((QUARTER, 2 * NB), BF16),
        ),
        grid=(1,),
        in_specs=[whole()] * 4 + [mark_rows()] * 4,
        out_specs=(whole(), whole()),
        cost_estimate=cost(0, 4 * NB * NB),
        name="slab_sum",
    )(*rs, *marks)
    got_slab = hop(sent_slab, 4)
    return pl.pallas_call(
        last_kernel,
        out_shape=jax.ShapeDtypeStruct((QUARTER, 6 * NB), F32),
        in_specs=[whole()] * 4,
        out_specs=whole(),
        cost_estimate=cost(0, 10 * NB * NB),
        name="last",
    )(kept_iface, got_iface, kept_slab, got_slab)


def solution(mesh):
    in_specs = (
        P(("grp", "dev"), None, None, None),
        P(("grp", "dev"), None, None, None),
        P(("grp", "dev"), None),
        P(("grp", "dev")),
        P(("grp", "dev")),
        P(("grp", "dev"), None, None),
    )
    out_specs = P(("grp", "dev"), None)
    on_device = on_square if mesh.shape["dev"] == 8 else on_any_slab
    return jax.shard_map(
        on_device, mesh=mesh, in_specs=in_specs, out_specs=out_specs, check_vma=False
    )
```

```python
import jax
import jax.numpy as jnp
from jax import lax
from jax.experimental import pallas as pl
from jax.experimental.pallas import tpu as pltpu
from jax.sharding import PartitionSpec as P

NB = 384
SLOTS = 6
REACH = 3
COARSE = 2
QUARTER = NB // 4
HALF = NB // 2
META = 16
TURNS = (0, 1, 2, 3, 5, 6, 7)
F32 = jnp.float32
BF16 = jnp.bfloat16


def passed_along(block, axis, distance):
    devices = range(lax.axis_size(axis))
    route = [((i - distance) % len(devices), i) for i in devices]
    return lax.ppermute(block, axis, route)


def extended(array, sides, width):
    for axis, dim in sides:
        count, length = (lax.axis_size(axis), array.shape[dim])
        up = [(i, (i + 1) % count) for i in range(count - 1)]
        down = [(j, i) for i, j in up]
        last = lax.slice_in_dim(array, length - width, length, axis=dim)
        initial = lax.slice_in_dim(array, 0, width, axis=dim)
        before = lax.ppermute(last, axis, up)
        after = lax.ppermute(initial, axis, down)
        array = jnp.concatenate([before, array, after], axis=dim)
    return array


def on_any_slab(stiff_rows, stiff_iface, columns, live_count, aggregate, prolong):
    dev_count = lax.axis_size("dev")
    grp_count = lax.axis_size("grp")
    group_at = lax.axis_index("grp")
    place_at = lax.axis_index("dev")
    my_columns = columns[0]
    block_list = []
    agg_list = []
    for offset in range(-REACH, REACH + 1):
        if offset == 0:
            block_list.append(prolong)
            agg_list.append(aggregate)
        else:
            got = passed_along((prolong, aggregate), "dev", -offset)
            block_list.append(got[0])
            agg_list.append(got[1])
    window_blocks = jnp.concatenate(block_list, axis=0)
    window_aggs = jnp.concatenate(agg_list, axis=0)
    offsets = (my_columns - place_at + dev_count + REACH) % dev_count
    panels = jnp.take(window_blocks, offsets, axis=0)
    column_aggs = jnp.take(window_aggs, offsets, axis=0)
    slab_blocks, slab_aggs = (
        extended(prolong, (("grp", 0),), 1),
        extended(aggregate, (("grp", 0),), 1),
    )
    blocks = jnp.concatenate([panels, slab_blocks[0:1], slab_blocks[2:3]], axis=0)
    stiff = jnp.concatenate([stiff_rows[0], stiff_iface[0]], axis=0)
    qmat = jnp.einsum("kfg,kgm->kfm", stiff, blocks, preferred_element_type=F32).astype(BF16)
    contrib = jnp.einsum("fc,kfm->kcm", prolong[0], qmat, preferred_element_type=F32)
    targets = jnp.concatenate([column_aggs, slab_aggs[0][None], slab_aggs[2][None]])
    weights = jnp.concatenate(
        [
            (jnp.arange(SLOTS, dtype=jnp.int32) < live_count[0]).astype(F32),
            (group_at > 0).astype(F32)[None],
            (group_at < grp_count - 1).astype(F32)[None],
        ]
    )
    sides = jnp.concatenate([jnp.ones((SLOTS,), jnp.int32), jnp.array([0, 2], jnp.int32)])
    side_hot = (sides[:, None] == jnp.arange(3, dtype=jnp.int32)[None, :]).astype(F32)
    block_hot = (targets[:, None] == jnp.arange(COARSE, dtype=jnp.int32)[None, :]).astype(F32)
    placing = side_hot[:, :, None] * block_hot[:, None, :] * weights[:, None, None]
    partial_value = jnp.einsum("ksb,kcm->csbm", placing, contrib).reshape(NB, 3 * COARSE * NB)
    partial_value = partial_value.astype(BF16).astype(F32)
    own_hot = (jnp.arange(COARSE, dtype=jnp.int32) == aggregate[0]).astype(F32)
    spread = (own_hot[:, None, None] * partial_value[None]).reshape(COARSE * NB, 3 * COARSE * NB)
    return lax.psum_scatter(
        spread.astype(BF16), "dev", scatter_dimension=0, tiled=True
    ).astype(F32)


def dot(a, b):
    return jnp.dot(a, b, preferred_element_type=F32)


def left_kernel(rows, iface, own, left, left_iface):
    turned = own[:NB].T
    for s in range(2):
        left_iface[s] = dot(turned, iface[0, s]).astype(BF16)
    for k in range(SLOTS):
        left[k] = dot(turned, rows[0, k]).astype(BF16)


def iface_kernel(left_iface, below, above, own, here, away, held):
    core = lax.axis_index("dev") % 2
    for s, block in enumerate((below, above)):
        held[s] = dot(left_iface[s], block[:NB]).astype(BF16)
    for x in range(2):
        for s in range(2):
            for c, out in ((core, here), (1 - core, away)):
                start = pl.multiple_of((2 * x + c) * QUARTER, QUARTER)
                out[(2 * x + s) * QUARTER : (2 * x + s + 1) * QUARTER] = held[s, pl.ds(start, QUARTER)]
    row = lax.broadcasted_iota(jnp.int32, (META, NB), 0)
    marks = jnp.zeros((META, NB), F32)
    for n, block in enumerate((below, above, own)):
        marks = jnp.where(row == n, block[NB:].astype(F32), marks)
    for out in (here, away):
        out[4 * QUARTER :] = marks.astype(BF16)


def row_marks(block, n):
    return block[4 * QUARTER + n : 4 * QUARTER + n + 1].astype(F32)


def pack_kernel(here, got, ours, there, kept, sent):
    place = lax.axis_index("dev")
    column, line = (place // 2) % 2, (place // 4).astype(F32)
    for x, out in ((column, ours), (1 - column, there)):
        start = pl.multiple_of(2 * x * QUARTER, QUARTER)
        for r, source in enumerate((here, got)):
            out[r * QUARTER : (r + 1) * QUARTER] = source[pl.ds(start, QUARTER)]
        row = lax.broadcasted_iota(jnp.int32, (META, NB), 0)
        marks = jnp.zeros((META, NB), F32)
        for r, source in enumerate((here, got)):
            for n, m in ((r, 0), (2 + r, 2)):
                marks = jnp.where(row == n, row_marks(source, m), marks)
        out[HALF:] = marks.astype(BF16)
    for a, out in ((line, kept), (1.0 - line, sent)):
        for b in range(COARSE):
            weights = []
            for source in (here, got):
                mark, into = row_marks(source, 2), row_marks(source, 1)
                weights.append((mark * a + (1.0 - mark) * (1.0 - a)) * (into if b else 1.0 - into))
            for x in range(2):
                at = (2 * x + 1) * QUARTER
                parts = [source[at : at + QUARTER].astype(F32) * w for source, w in zip((here, got), weights)]
                out[x * QUARTER : (x + 1) * QUARTER, b * NB : (b + 1) * NB] = (parts[0] + parts[1]).astype(out.dtype)


def below_sum_kernel(ours, theirs, kept, sent):
    line = (lax.axis_index("dev") // 4).astype(F32)
    marks = [v[HALF:].astype(F32) for v in (ours, theirs)]
    for a, out in ((line, kept), (1.0 - line, sent)):
        for b in range(COARSE):
            total = None
            for v, mark in zip((ours, theirs), marks):
                for r in range(2):
                    row_mark, into = mark[2 + r : 3 + r], mark[r : r + 1]
                    weight = (row_mark * a + (1.0 - row_mark) * (1.0 - a)) * (into if b else 1.0 - into)
                    value = v[r * QUARTER : (r + 1) * QUARTER].astype(F32) * weight
                    total = value if total is None else total + value
            out[:, b * NB : (b + 1) * NB] = total.astype(out.dtype)


def above_sum_kernel(ours, got, kept, sent):
    column = (lax.axis_index("dev") // 2) % 2
    for x, out in ((column, kept), (1 - column, sent)):
        at = pl.ds(pl.multiple_of(x * QUARTER, QUARTER), QUARTER)
        out[...] = (ours[at] + got[at].astype(F32)).astype(out.dtype)


def slab_kernel(columns, live, left, b0, b1, b2, b3, b5, b6, b7, kept, sent, held):
    place = lax.axis_index("dev")
    core = place % 2
    held[...] = jnp.zeros_like(held)
    for t, block in zip(TURNS, (b0, b1, b2, b3, b5, b6, b7)):
        slot = jnp.int32(SLOTS)
        for k in range(SLOTS):
            slot = jnp.where((columns[0, k] ^ place) == t, k, slot)

        @pl.when(slot < live[0])
        def _():
            value = dot(left[slot], block[:NB])
            upper = block[NB : NB + 1].astype(F32)
            held[0] += value * (1.0 - upper)
            held[1] += value * upper

    for c, out in ((core, kept), (1 - core, sent)):
        for x in range(2):
            start = pl.multiple_of((2 * x + c) * QUARTER, QUARTER)
            for b in range(COARSE):
                value = held[b, pl.ds(start, QUARTER)]
                out[x * QUARTER : (x + 1) * QUARTER, b * NB : (b + 1) * NB] = value.astype(out.dtype)


def slab_sum_kernel(ours, got, b0, b1, kept, s2, s4, s6):
    place = lax.axis_index("dev")
    column, line = (place // 2) % 2, place // 4
    side = line.astype(F32)
    for a, outs in ((side, (kept, s2)), (1.0 - side, (s4, s6))):
        weights = []
        for block in (b0, b1):
            mark = block[NB : NB + 1].astype(F32)
            mark = jnp.concatenate([mark, mark], axis=1)
            weights.append(mark * a + (1.0 - mark) * (1.0 - a))
        for x, out in zip((column, 1 - column), outs):
            at = pl.ds(pl.multiple_of(x * QUARTER, QUARTER), QUARTER)
            out[...] = (ours[at] * weights[0] + got[at].astype(F32) * weights[1]).astype(out.dtype)


def last_kernel(below, got_below, kept, r2, r4, r6, above, got_above, out):
    wide = COARSE * NB
    out[:, :wide] = below[...] + got_below[...].astype(F32)
    out[:, wide : 2 * wide] = kept[...] + r2[...].astype(F32) + r4[...].astype(F32) + r6[...].astype(F32)
    out[:, 2 * wide :] = above[...] + got_above[...].astype(F32)


def whole():
    return pl.BlockSpec(memory_space=pltpu.VMEM)


def scalars():
    return pl.BlockSpec(memory_space=pltpu.SMEM)


def call(kernel, name, outs, in_specs, scratch=(), limit=16):
    return pl.pallas_call(
        kernel,
        out_shape=tuple(jax.ShapeDtypeStruct(shape, kind) for shape, kind in outs),
        in_specs=in_specs,
        out_specs=(whole(),) * len(outs),
        scratch_shapes=scratch,
        compiler_params=pltpu.CompilerParams(vmem_limit_bytes=limit * 2**20),
        name=name,
    )


def after(value, *others):
    return lax.optimization_barrier((value, *others))[0]


def on_square(stiff_rows, stiff_iface, columns, live_count, aggregate, prolong):
    groups = lax.axis_size("grp")
    up = [(i, i + 1) for i in range(groups - 1)]
    down = [(j, i) for i, j in up]

    def hop(block, turn):
        return lax.ppermute(block, "dev", [(i, i ^ turn) for i in range(8)])

    block_row = lax.broadcasted_iota(jnp.int32, (NB + META, NB), 0) < NB
    longer = jnp.pad(prolong[0], ((0, META), (0, 0)))
    own = jnp.where(block_row, longer, aggregate.astype(BF16)[:, None])
    b5 = hop(own, 5)
    b2 = hop(own, 2)
    below = lax.ppermute(own, "grp", up)
    above = lax.ppermute(own, "grp", down)
    b7 = hop(b5, 2)

    columns, live_count = after((columns, live_count), b2)
    left, left_iface = call(left_kernel, "left", (((SLOTS, NB, NB), BF16), ((2, NB, NB), BF16)), [whole()] * 3)(
        stiff_rows, stiff_iface, after(own, b2, b5)
    )
    row = ((4 * QUARTER + META, NB), BF16)
    here, away = call(iface_kernel, "iface", (row, row), [whole()] * 4, [pltpu.VMEM((2, NB, NB), BF16)])(
        left_iface, below, above, own
    )
    got_here = hop(away, 1)
    b1 = hop(after(own, here), 1)
    b3 = hop(after(b2, here), 1)
    b6 = hop(after(b7, here), 1)

    wide = COARSE * NB
    packed = (HALF + META, NB)
    ours, there, line_kept, line_sent = call(
        pack_kernel, "pack", ((packed, BF16), (packed, BF16), ((HALF, wide), F32), ((HALF, wide), BF16)), [whole()] * 2
    )(here, got_here)
    got_line = hop(line_sent, 4)
    theirs = hop(there, 2)

    kept, sent = call(
        slab_kernel,
        "slab",
        (((HALF, wide), F32), ((HALF, wide), BF16)),
        [scalars(), scalars()] + [whole()] * 8,
        [pltpu.VMEM((COARSE, NB, NB), F32)],
    )(columns, live_count, left, own, b1, b2, b3, b5, b6, b7)
    got_slab = hop(sent, 1)
    part = (QUARTER, wide)
    kept, s2, s4, s6 = call(
        slab_sum_kernel, "slab_sum", ((part, F32), (part, BF16), (part, BF16), (part, BF16)), [whole()] * 4
    )(kept, got_slab, own, b1)
    r2, r4, r6 = hop(s2, 2), hop(s4, 4), hop(s6, 6)

    pair = ((part, F32), (part, BF16))
    below_kept, below_sent = call(below_sum_kernel, "below_sum", pair, [whole()] * 2)(ours, after(theirs, s2, s4, s6))
    got_below = hop(below_sent, 4)
    above_kept, above_sent = call(above_sum_kernel, "above_sum", pair, [whole()] * 2)(line_kept, after(got_line, s2, s4, s6))
    got_above = hop(above_sent, 2)
    return call(last_kernel, "last", (((QUARTER, 3 * wide), F32),), [whole()] * 8)(
        below_kept, got_below, kept, r2, r4, r6, above_kept, got_above
    )[0]


def solution(mesh):
    in_specs = (
        P(("grp", "dev"), None, None, None),
        P(("grp", "dev"), None, None, None),
        P(("grp", "dev"), None),
        P(("grp", "dev")),
        P(("grp", "dev")),
        P(("grp", "dev"), None, None),
    )
    out_specs = P(("grp", "dev"), None)
    on_device = on_square if mesh.shape["dev"] == 8 else on_any_slab
    return jax.shard_map(
        on_device, mesh=mesh, in_specs=in_specs, out_specs=out_specs, check_vma=False
    )
```

```python
import jax
import jax.numpy as jnp
from jax import lax
from jax.experimental import pallas as pl
from jax.experimental.pallas import tpu as pltpu
from jax.sharding import PartitionSpec as P

NB = 384
SLOTS = 6
REACH = 3
COARSE = 2
QUARTER = NB // 4
HALF = NB // 2
META = 16
MARKED = NB + META
TURNS = (0, 1, 2, 3, 5, 6, 7)
WEIGHT = {'own': 4000000000, 'left': 1000000000, 'iface': 4000000000, 'pack': 4000000000, 'slab': 4000000000, 'slab_sum': 4000000000, 'below_sum': 4000000000, 'above_sum': 4000000000, 'last': 4000000000}
F32 = jnp.float32
BF16 = jnp.bfloat16


def passed_along(block, axis, distance):
    devices = range(lax.axis_size(axis))
    route = [((i - distance) % len(devices), i) for i in devices]
    return lax.ppermute(block, axis, route)


def extended(array, sides, width):
    for axis, dim in sides:
        count, length = (lax.axis_size(axis), array.shape[dim])
        up = [(i, (i + 1) % count) for i in range(count - 1)]
        down = [(j, i) for i, j in up]
        last = lax.slice_in_dim(array, length - width, length, axis=dim)
        initial = lax.slice_in_dim(array, 0, width, axis=dim)
        before = lax.ppermute(last, axis, up)
        after = lax.ppermute(initial, axis, down)
        array = jnp.concatenate([before, array, after], axis=dim)
    return array


def on_any_slab(stiff_rows, stiff_iface, columns, live_count, aggregate, prolong):
    dev_count = lax.axis_size("dev")
    grp_count = lax.axis_size("grp")
    group_at = lax.axis_index("grp")
    place_at = lax.axis_index("dev")
    my_columns = columns[0]
    block_list = []
    agg_list = []
    for offset in range(-REACH, REACH + 1):
        if offset == 0:
            block_list.append(prolong)
            agg_list.append(aggregate)
        else:
            got = passed_along((prolong, aggregate), "dev", -offset)
            block_list.append(got[0])
            agg_list.append(got[1])
    window_blocks = jnp.concatenate(block_list, axis=0)
    window_aggs = jnp.concatenate(agg_list, axis=0)
    offsets = (my_columns - place_at + dev_count + REACH) % dev_count
    panels = jnp.take(window_blocks, offsets, axis=0)
    column_aggs = jnp.take(window_aggs, offsets, axis=0)
    slab_blocks, slab_aggs = (
        extended(prolong, (("grp", 0),), 1),
        extended(aggregate, (("grp", 0),), 1),
    )
    blocks = jnp.concatenate([panels, slab_blocks[0:1], slab_blocks[2:3]], axis=0)
    stiff = jnp.concatenate([stiff_rows[0], stiff_iface[0]], axis=0)
    qmat = jnp.einsum("kfg,kgm->kfm", stiff, blocks, preferred_element_type=F32).astype(BF16)
    contrib = jnp.einsum("fc,kfm->kcm", prolong[0], qmat, preferred_element_type=F32)
    targets = jnp.concatenate([column_aggs, slab_aggs[0][None], slab_aggs[2][None]])
    weights = jnp.concatenate(
        [
            (jnp.arange(SLOTS, dtype=jnp.int32) < live_count[0]).astype(F32),
            (group_at > 0).astype(F32)[None],
            (group_at < grp_count - 1).astype(F32)[None],
        ]
    )
    sides = jnp.concatenate([jnp.ones((SLOTS,), jnp.int32), jnp.array([0, 2], jnp.int32)])
    side_hot = (sides[:, None] == jnp.arange(3, dtype=jnp.int32)[None, :]).astype(F32)
    block_hot = (targets[:, None] == jnp.arange(COARSE, dtype=jnp.int32)[None, :]).astype(F32)
    placing = side_hot[:, :, None] * block_hot[:, None, :] * weights[:, None, None]
    partial_value = jnp.einsum("ksb,kcm->csbm", placing, contrib).reshape(NB, 3 * COARSE * NB)
    partial_value = partial_value.astype(BF16).astype(F32)
    own_hot = (jnp.arange(COARSE, dtype=jnp.int32) == aggregate[0]).astype(F32)
    spread = (own_hot[:, None, None] * partial_value[None]).reshape(COARSE * NB, 3 * COARSE * NB)
    return lax.psum_scatter(
        spread.astype(BF16), "dev", scatter_dimension=0, tiled=True
    ).astype(F32)


def dot(a, b):
    return jnp.dot(a, b, preferred_element_type=F32)


def own_kernel(aggregate, prolong, own):
    own[:NB] = prolong[0]
    own[NB:] = jnp.broadcast_to(aggregate[...], (META, NB)).astype(F32).astype(BF16)


def left_kernel(columns, live, rows, iface, own, left, left_iface):
    place = lax.axis_index("dev")
    turned = own[:NB].T
    for s in range(2):
        left_iface[s] = dot(turned, iface[0, s]).astype(BF16)
    left[...] = jnp.zeros_like(left)
    for k in range(SLOTS):

        @pl.when(k < live[0])
        def _():
            left[columns[0, k] ^ place] = dot(turned, rows[0, k]).astype(BF16)


def iface_kernel(left_iface, below, above, own, here0, here1, away0, away1, held):
    core = lax.axis_index("dev") % 2
    row = lax.broadcasted_iota(jnp.int32, (META, NB), 0)
    for s, (block, here, away) in enumerate(((below, here0, away0), (above, here1, away1))):
        held[s] = dot(left_iface[s], block[:NB]).astype(BF16)
        marks = jnp.where(row == 0, block[NB:].astype(F32), own[NB:].astype(F32)).astype(BF16)
        for c, out in ((core, here), (1 - core, away)):
            for x in range(2):
                start = pl.multiple_of((2 * x + c) * QUARTER, QUARTER)
                out[x * QUARTER : (x + 1) * QUARTER] = held[s, pl.ds(start, QUARTER)]
            out[HALF:] = marks


def row_marks(block, n):
    return block[HALF:].astype(F32)[n : n + 1]


def pack_kernel(here0, here1, got0, got1, ours, there, kept, sent):
    place = lax.axis_index("dev")
    column, line = (place // 2) % 2, (place // 4).astype(F32)
    row = lax.broadcasted_iota(jnp.int32, (META, NB), 0)
    marks = jnp.zeros((META, NB), F32)
    for r, source in enumerate((here0, got0)):
        for n, m in ((r, 0), (2 + r, 1)):
            marks = jnp.where(row == n, row_marks(source, m), marks)
    for x, out in ((column, ours), (1 - column, there)):
        start = pl.multiple_of(x * QUARTER, QUARTER)
        for r, source in enumerate((here0, got0)):
            out[r * QUARTER : (r + 1) * QUARTER] = source[pl.ds(start, QUARTER)]
        out[HALF:] = marks.astype(BF16)
    for a, out in ((line, kept), (1.0 - line, sent)):
        for b in range(COARSE):
            total = 0.0
            for source in (here1, got1):
                into, mark = row_marks(source, 0), row_marks(source, 1)
                weight = (mark * a + (1.0 - mark) * (1.0 - a)) * (into if b else 1.0 - into)
                total = total + source[:HALF].astype(F32) * weight
            out[:, b * NB : (b + 1) * NB] = total.astype(out.dtype)


def below_sum_kernel(ours, theirs, kept, sent):
    line = (lax.axis_index("dev") // 4).astype(F32)
    marks = [v[HALF:].astype(F32) for v in (ours, theirs)]
    for a, out in ((line, kept), (1.0 - line, sent)):
        for b in range(COARSE):
            total = None
            for v, mark in zip((ours, theirs), marks):
                for r in range(2):
                    row_mark, into = mark[2 + r : 3 + r], mark[r : r + 1]
                    weight = (row_mark * a + (1.0 - row_mark) * (1.0 - a)) * (into if b else 1.0 - into)
                    value = v[r * QUARTER : (r + 1) * QUARTER].astype(F32) * weight
                    total = value if total is None else total + value
            out[:, b * NB : (b + 1) * NB] = total.astype(out.dtype)


def above_sum_kernel(ours, got, kept, sent):
    column = (lax.axis_index("dev") // 2) % 2
    for x, out in ((column, kept), (1 - column, sent)):
        at = pl.ds(pl.multiple_of(x * QUARTER, QUARTER), QUARTER)
        out[...] = (ours[at] + got[at].astype(F32)).astype(out.dtype)


def slab_kernel(left, b0, b1, b2, b3, b5, b6, b7, kept, sent0, sent1, held):
    core = lax.axis_index("dev") % 2
    for t, block in zip(TURNS, (b0, b1, b2, b3, b5, b6, b7)):
        value = dot(left[t], block[:NB])
        upper = block[NB:].astype(F32)[:1]
        for b, weight in enumerate((1.0 - upper, upper)):
            held[b] = value * weight if t == 0 else held[b] + value * weight
    for x in range(2):
        for b, sent in enumerate((sent0, sent1)):
            start = pl.multiple_of((2 * x + core) * QUARTER, QUARTER)
            kept[x * QUARTER : (x + 1) * QUARTER, b * NB : (b + 1) * NB] = held[b, pl.ds(start, QUARTER)]
            start = pl.multiple_of((2 * x + 1 - core) * QUARTER, QUARTER)
            sent[x * QUARTER : (x + 1) * QUARTER] = held[b, pl.ds(start, QUARTER)].astype(BF16)


def slab_sum_kernel(ours, got0, got1, b0, b1, kept, s2, s4, s6):
    place = lax.axis_index("dev")
    column, line = (place // 2) % 2, place // 4
    side = line.astype(F32)
    for a, outs in ((side, (kept, s2)), (1.0 - side, (s4, s6))):
        weights = []
        for block in (b0, b1):
            mark = block[NB:].astype(F32)[:1]
            weights.append(mark * a + (1.0 - mark) * (1.0 - a))
        for x, out in zip((column, 1 - column), outs):
            at = pl.ds(pl.multiple_of(x * QUARTER, QUARTER), QUARTER)
            for b, got in enumerate((got0, got1)):
                cut = slice(b * NB, (b + 1) * NB)
                out[:, cut] = (ours[at, cut] * weights[0] + got[at].astype(F32) * weights[1]).astype(out.dtype)


def last_kernel(below, got_below, kept, r2, r4, r6, above, got_above, out, held, sems):
    wide = COARSE * NB
    copies = []
    for side, parts in ((0, (below, got_below)), (2, (above, got_above)), (1, (kept, r2, r4, r6))):
        total = parts[0][...]
        for part in parts[1:]:
            total = total + part[...].astype(F32)
        held[side] = total
        copies.append(pltpu.make_async_copy(held.at[side], out.at[:, pl.ds(side * wide, wide)], sems.at[side]))
        copies[-1].start()
    for copy in copies:
        copy.wait()


def whole():
    return pl.BlockSpec(memory_space=pltpu.VMEM)


def scalars():
    return pl.BlockSpec(memory_space=pltpu.SMEM)


def call(kernel, name, outs, in_specs, scratch=(), out_specs=None):
    weight = WEIGHT.get(name)
    return pl.pallas_call(
        kernel,
        out_shape=tuple(jax.ShapeDtypeStruct(shape, kind) for shape, kind in outs),
        in_specs=in_specs,
        out_specs=out_specs or (whole(),) * len(outs),
        scratch_shapes=scratch,
        compiler_params=pltpu.CompilerParams(vmem_limit_bytes=16 * 2**20),
        cost_estimate=pl.CostEstimate(flops=weight, bytes_accessed=1000, transcendentals=0) if weight is not None else None,
        name=name,
    )


def after(value, *others):
    return lax.optimization_barrier((value, *others))[0]


def on_square(stiff_rows, stiff_iface, columns, live_count, aggregate, prolong):
    groups = lax.axis_size("grp")
    up = [(i, i + 1) for i in range(groups - 1)]
    down = [(j, i) for i, j in up]
    wide = COARSE * NB
    part, block, half = (QUARTER, wide), (MARKED, NB), (HALF + META, NB)

    def hop(array, turn):
        return lax.ppermute(array, "dev", [(i, i ^ turn) for i in range(8)])

    own = call(own_kernel, "own", ((block, BF16),), [whole()] * 2)(aggregate.reshape(1, 1), prolong)[0]
    b5 = hop(own, 5)
    b2 = hop(own, 2)
    below = lax.ppermute(own, "grp", up)
    above = lax.ppermute(own, "grp", down)
    b6 = hop(own, 6)
    columns, live_count = after((columns, live_count), b6)
    left, left_iface = call(
        left_kernel, "left", (((8, NB, NB), BF16), ((2, NB, NB), BF16)), [scalars()] * 2 + [whole()] * 3
    )(columns, live_count, stiff_rows, stiff_iface, own)
    here0, here1, away0, away1 = call(
        iface_kernel, "iface", ((half, BF16),) * 4, [whole()] * 4, [pltpu.VMEM((2, NB, NB), BF16)]
    )(left_iface, below, above, own)
    got0, got1 = hop(away0, 1), hop(away1, 1)
    ours, there, line_kept, line_sent = call(
        pack_kernel, "pack", ((half, BF16), (half, BF16), ((HALF, wide), F32), ((HALF, wide), BF16)), [whole()] * 4
    )(here0, here1, got0, after(got1, b5))
    theirs = hop(there, 2)
    below_kept, below_sent = call(below_sum_kernel, "below_sum", ((part, F32), (part, BF16)), [whole()] * 2)(
        ours, theirs
    )
    got_below = hop(below_sent, 4)
    b1 = hop(own, 1)
    b3 = hop(b2, 1)
    b7 = hop(after(b6, here0), 1)
    kept, sent0, sent1 = call(
        slab_kernel,
        "slab",
        (((HALF, wide), F32), ((HALF, NB), BF16), ((HALF, NB), BF16)),
        [whole()] * 8,
        [pltpu.VMEM((COARSE, NB, NB), F32)],
    )(left, own, b1, b2, b3, b5, b6, b7)
    sent = hop(sent0, 1), hop(sent1, 1)
    sum_kept, s2, s4, s6 = call(
        slab_sum_kernel, "slab_sum", ((part, F32), (part, BF16), (part, BF16), (part, BF16)), [whole()] * 5
    )(kept, sent[0], sent[1], own, b1)
    r2, r4, r6 = hop(s2, 2), hop(s4, 4), hop(s6, 6)
    got_line = hop(line_sent, 4)
    above_kept, above_sent = call(above_sum_kernel, "above_sum", ((part, F32), (part, BF16)), [whole()] * 2)(
        line_kept, got_line
    )
    got_above = hop(above_sent, 2)
    return call(
        last_kernel,
        "last",
        (((QUARTER, 3 * wide), F32),),
        [whole()] * 8,
        [pltpu.VMEM((3, QUARTER, wide), F32), pltpu.SemaphoreType.DMA((3,))],
        (pl.BlockSpec(memory_space=pltpu.HBM),),
    )(below_kept, got_below, sum_kept, r2, r4, r6, above_kept, got_above)[0]


def solution(mesh):
    in_specs = (
        P(("grp", "dev"), None, None, None),
        P(("grp", "dev"), None, None, None),
        P(("grp", "dev"), None),
        P(("grp", "dev")),
        P(("grp", "dev")),
        P(("grp", "dev"), None, None),
    )
    out_specs = P(("grp", "dev"), None)
    on_device = on_square if mesh.shape["dev"] == 8 else on_any_slab
    return jax.shard_map(
        on_device, mesh=mesh, in_specs=in_specs, out_specs=out_specs, check_vma=False
    )
```

```python
import jax
import jax.numpy as jnp
from jax import lax
from jax.experimental import pallas as pl
from jax.experimental.pallas import tpu as pltpu
from jax.sharding import PartitionSpec as P

NB = 384
SLOTS = 6
REACH = 3
COARSE = 2
QUARTER = NB // 4
HALF = NB // 2
META = 16
MARKED = NB + META
TURNS = (0, 1, 2, 3, 5, 6, 7)
WEIGHT = {'own': 4000000000, 'left': 1000000000, 'iface': 4000000000, 'pack': 4000000000, 'slab': 4000000000, 'slab_sum': 4000000000, 'below_sum': 4000000000, 'above_sum': 4000000000, 'last': 4000000000}
F32 = jnp.float32
BF16 = jnp.bfloat16


def passed_along(block, axis, distance):
    devices = range(lax.axis_size(axis))
    route = [((i - distance) % len(devices), i) for i in devices]
    return lax.ppermute(block, axis, route)


def extended(array, sides, width):
    for axis, dim in sides:
        count, length = (lax.axis_size(axis), array.shape[dim])
        up = [(i, (i + 1) % count) for i in range(count - 1)]
        down = [(j, i) for i, j in up]
        last = lax.slice_in_dim(array, length - width, length, axis=dim)
        initial = lax.slice_in_dim(array, 0, width, axis=dim)
        before = lax.ppermute(last, axis, up)
        after = lax.ppermute(initial, axis, down)
        array = jnp.concatenate([before, array, after], axis=dim)
    return array


def on_any_slab(stiff_rows, stiff_iface, columns, live_count, aggregate, prolong):
    dev_count = lax.axis_size("dev")
    grp_count = lax.axis_size("grp")
    group_at = lax.axis_index("grp")
    place_at = lax.axis_index("dev")
    my_columns = columns[0]
    block_list = []
    agg_list = []
    for offset in range(-REACH, REACH + 1):
        if offset == 0:
            block_list.append(prolong)
            agg_list.append(aggregate)
        else:
            got = passed_along((prolong, aggregate), "dev", -offset)
            block_list.append(got[0])
            agg_list.append(got[1])
    window_blocks = jnp.concatenate(block_list, axis=0)
    window_aggs = jnp.concatenate(agg_list, axis=0)
    offsets = (my_columns - place_at + dev_count + REACH) % dev_count
    panels = jnp.take(window_blocks, offsets, axis=0)
    column_aggs = jnp.take(window_aggs, offsets, axis=0)
    slab_blocks, slab_aggs = (
        extended(prolong, (("grp", 0),), 1),
        extended(aggregate, (("grp", 0),), 1),
    )
    blocks = jnp.concatenate([panels, slab_blocks[0:1], slab_blocks[2:3]], axis=0)
    stiff = jnp.concatenate([stiff_rows[0], stiff_iface[0]], axis=0)
    qmat = jnp.einsum("kfg,kgm->kfm", stiff, blocks, preferred_element_type=F32).astype(BF16)
    contrib = jnp.einsum("fc,kfm->kcm", prolong[0], qmat, preferred_element_type=F32)
    targets = jnp.concatenate([column_aggs, slab_aggs[0][None], slab_aggs[2][None]])
    weights = jnp.concatenate(
        [
            (jnp.arange(SLOTS, dtype=jnp.int32) < live_count[0]).astype(F32),
            (group_at > 0).astype(F32)[None],
            (group_at < grp_count - 1).astype(F32)[None],
        ]
    )
    sides = jnp.concatenate([jnp.ones((SLOTS,), jnp.int32), jnp.array([0, 2], jnp.int32)])
    side_hot = (sides[:, None] == jnp.arange(3, dtype=jnp.int32)[None, :]).astype(F32)
    block_hot = (targets[:, None] == jnp.arange(COARSE, dtype=jnp.int32)[None, :]).astype(F32)
    placing = side_hot[:, :, None] * block_hot[:, None, :] * weights[:, None, None]
    partial_value = jnp.einsum("ksb,kcm->csbm", placing, contrib).reshape(NB, 3 * COARSE * NB)
    partial_value = partial_value.astype(BF16).astype(F32)
    own_hot = (jnp.arange(COARSE, dtype=jnp.int32) == aggregate[0]).astype(F32)
    spread = (own_hot[:, None, None] * partial_value[None]).reshape(COARSE * NB, 3 * COARSE * NB)
    return lax.psum_scatter(
        spread.astype(BF16), "dev", scatter_dimension=0, tiled=True
    ).astype(F32)


def dot(a, b):
    return jnp.dot(a, b, preferred_element_type=F32)


def own_kernel(aggregate, prolong, own, longer):
    mark = jnp.broadcast_to(aggregate[...], (META, NB)).astype(F32).astype(BF16)
    for out in (own, longer):
        out[:NB] = prolong[0]
        for start in range(NB, out.shape[0], META):
            out[start : start + META] = mark


def left_kernel(columns, live, rows, iface, own, left, left_iface):
    place = lax.axis_index("dev")
    turned = own[:NB].T
    for s in range(2):
        left_iface[s] = dot(turned, iface[0, s]).astype(BF16)
    left[...] = jnp.zeros_like(left)
    for k in range(SLOTS):

        @pl.when(k < live[0])
        def _():
            left[columns[0, k] ^ place] = dot(turned, rows[0, k]).astype(BF16)


def iface_kernel(left_iface, below, above, own, here0, here1, away0, away1, held):
    core = lax.axis_index("dev") % 2
    row = lax.broadcasted_iota(jnp.int32, (META, NB), 0)
    for s, (block, here, away) in enumerate(((below, here0, away0), (above, here1, away1))):
        held[s] = dot(left_iface[s], block[:NB]).astype(BF16)
        marks = jnp.where(row == 0, block[NB:MARKED].astype(F32), own[NB:].astype(F32)).astype(BF16)
        for c, out in ((core, here), (1 - core, away)):
            for x in range(2):
                start = pl.multiple_of((2 * x + c) * QUARTER, QUARTER)
                out[x * QUARTER : (x + 1) * QUARTER] = held[s, pl.ds(start, QUARTER)]
            out[HALF:] = marks


def row_marks(block, n):
    return block[HALF:].astype(F32)[n : n + 1]


def pack_kernel(here0, here1, got0, got1, ours, there, kept, sent):
    place = lax.axis_index("dev")
    column, line = (place // 2) % 2, (place // 4).astype(F32)
    row = lax.broadcasted_iota(jnp.int32, (META, NB), 0)
    marks = jnp.zeros((META, NB), F32)
    for r, source in enumerate((here0, got0)):
        for n, m in ((r, 0), (2 + r, 1)):
            marks = jnp.where(row == n, row_marks(source, m), marks)
    for x, out in ((column, ours), (1 - column, there)):
        start = pl.multiple_of(x * QUARTER, QUARTER)
        for r, source in enumerate((here0, got0)):
            out[r * QUARTER : (r + 1) * QUARTER] = source[pl.ds(start, QUARTER)]
        out[HALF:] = marks.astype(BF16)
    for a, out in ((line, kept), (1.0 - line, sent)):
        for b in range(COARSE):
            total = 0.0
            for source in (here1, got1):
                into, mark = row_marks(source, 0), row_marks(source, 1)
                weight = (mark * a + (1.0 - mark) * (1.0 - a)) * (into if b else 1.0 - into)
                total = total + source[:HALF].astype(F32) * weight
            out[:, b * NB : (b + 1) * NB] = total.astype(out.dtype)


def below_sum_kernel(ours, theirs, kept, sent):
    line = (lax.axis_index("dev") // 4).astype(F32)
    marks = [v[HALF:].astype(F32) for v in (ours, theirs)]
    for a, out in ((line, kept), (1.0 - line, sent)):
        for b in range(COARSE):
            total = None
            for v, mark in zip((ours, theirs), marks):
                for r in range(2):
                    row_mark, into = mark[2 + r : 3 + r], mark[r : r + 1]
                    weight = (row_mark * a + (1.0 - row_mark) * (1.0 - a)) * (into if b else 1.0 - into)
                    value = v[r * QUARTER : (r + 1) * QUARTER].astype(F32) * weight
                    total = value if total is None else total + value
            out[:, b * NB : (b + 1) * NB] = total.astype(out.dtype)


def above_sum_kernel(ours, got, kept, sent):
    column = (lax.axis_index("dev") // 2) % 2
    for x, out in ((column, kept), (1 - column, sent)):
        at = pl.ds(pl.multiple_of(x * QUARTER, QUARTER), QUARTER)
        out[...] = (ours[at] + got[at].astype(F32)).astype(out.dtype)


def slab_kernel(left, b0, b1, b2, b3, b5, b6, b7, kept, sent0, sent1, held):
    core = lax.axis_index("dev") % 2
    for t, block in zip(TURNS, (b0, b1, b2, b3, b5, b6, b7)):
        value = dot(left[t], block[:NB])
        upper = block[NB:].astype(F32)[:1]
        for b, weight in enumerate((1.0 - upper, upper)):
            held[b] = value * weight if t == 0 else held[b] + value * weight
    for x in range(2):
        for b, sent in enumerate((sent0, sent1)):
            start = pl.multiple_of((2 * x + core) * QUARTER, QUARTER)
            kept[x * QUARTER : (x + 1) * QUARTER, b * NB : (b + 1) * NB] = held[b, pl.ds(start, QUARTER)]
            start = pl.multiple_of((2 * x + 1 - core) * QUARTER, QUARTER)
            sent[x * QUARTER : (x + 1) * QUARTER] = held[b, pl.ds(start, QUARTER)].astype(BF16)


def slab_sum_kernel(ours, got0, got1, b0, b1, kept, s2, s4, s6):
    place = lax.axis_index("dev")
    column, line = (place // 2) % 2, place // 4
    side = line.astype(F32)
    for a, outs in ((side, (kept, s2)), (1.0 - side, (s4, s6))):
        weights = []
        for block in (b0, b1):
            mark = block[NB:].astype(F32)[:1]
            weights.append(mark * a + (1.0 - mark) * (1.0 - a))
        for x, out in zip((column, 1 - column), outs):
            at = pl.ds(pl.multiple_of(x * QUARTER, QUARTER), QUARTER)
            for b, got in enumerate((got0, got1)):
                cut = slice(b * NB, (b + 1) * NB)
                out[:, cut] = (ours[at, cut] * weights[0] + got[at].astype(F32) * weights[1]).astype(out.dtype)


def last_kernel(below, got_below, kept, r2, r4, r6, above, got_above, out, held, sems):
    wide = COARSE * NB
    copies = []
    for side, parts in ((0, (below, got_below)), (2, (above, got_above)), (1, (kept, r2, r4, r6))):
        total = parts[0][...]
        for part in parts[1:]:
            total = total + part[...].astype(F32)
        held[side] = total
        copies.append(pltpu.make_async_copy(held.at[side], out.at[:, pl.ds(side * wide, wide)], sems.at[side]))
        copies[-1].start()
    for copy in copies:
        copy.wait()


def whole():
    return pl.BlockSpec(memory_space=pltpu.VMEM)


def scalars():
    return pl.BlockSpec(memory_space=pltpu.SMEM)


def call(kernel, name, outs, in_specs, scratch=(), out_specs=None):
    weight = WEIGHT.get(name)
    return pl.pallas_call(
        kernel,
        out_shape=tuple(jax.ShapeDtypeStruct(shape, kind) for shape, kind in outs),
        in_specs=in_specs,
        out_specs=out_specs or (whole(),) * len(outs),
        scratch_shapes=scratch,
        compiler_params=pltpu.CompilerParams(vmem_limit_bytes=16 * 2**20),
        cost_estimate=pl.CostEstimate(flops=weight, bytes_accessed=1000, transcendentals=0) if weight is not None else None,
        name=name,
    )


def after(value, *others):
    return lax.optimization_barrier((value, *others))[0]


def on_square(stiff_rows, stiff_iface, columns, live_count, aggregate, prolong):
    groups = lax.axis_size("grp")
    up = [(i, i + 1) for i in range(groups - 1)]
    down = [(j, i) for i, j in up]
    wide = COARSE * NB
    part, block, half = (QUARTER, wide), (MARKED, NB), (HALF + META, NB)

    def hop(array, turn):
        return lax.ppermute(array, "dev", [(i, i ^ turn) for i in range(8)])

    own, longer = call(own_kernel, "own", ((block, BF16), ((MARKED + META, NB), BF16)), [whole()] * 2)(
        aggregate.reshape(1, 1), prolong
    )
    b5 = hop(own, 5)
    b2 = hop(own, 2)
    below = lax.ppermute(longer, "grp", up)
    above = lax.ppermute(own, "grp", down)
    b6 = hop(own, 6)
    columns, live_count = after((columns, live_count), b6)
    left, left_iface = call(
        left_kernel, "left", (((8, NB, NB), BF16), ((2, NB, NB), BF16)), [scalars()] * 2 + [whole()] * 3
    )(columns, live_count, stiff_rows, stiff_iface, own)
    here0, here1, away0, away1 = call(
        iface_kernel, "iface", ((half, BF16),) * 4, [whole()] * 4, [pltpu.VMEM((2, NB, NB), BF16)]
    )(left_iface, below, above, own)
    got0, got1 = hop(away0, 1), hop(away1, 1)
    ours, there, line_kept, line_sent = call(
        pack_kernel, "pack", ((half, BF16), (half, BF16), ((HALF, wide), F32), ((HALF, wide), BF16)), [whole()] * 4
    )(here0, here1, got0, after(got1, b5))
    theirs = hop(there, 2)
    below_kept, below_sent = call(below_sum_kernel, "below_sum", ((part, F32), (part, BF16)), [whole()] * 2)(
        ours, theirs
    )
    got_below = hop(below_sent, 4)
    b1 = hop(own, 1)
    b3 = hop(b2, 1)
    b7 = hop(after(b6, here0), 1)
    kept, sent0, sent1 = call(
        slab_kernel,
        "slab",
        (((HALF, wide), F32), ((HALF, NB), BF16), ((HALF, NB), BF16)),
        [whole()] * 8,
        [pltpu.VMEM((COARSE, NB, NB), F32)],
    )(left, own, b1, b2, b3, b5, b6, b7)
    sent = hop(sent0, 1), hop(sent1, 1)
    sum_kept, s2, s4, s6 = call(
        slab_sum_kernel, "slab_sum", ((part, F32), (part, BF16), (part, BF16), (part, BF16)), [whole()] * 5
    )(kept, sent[0], sent[1], own, b1)
    r2, r4, r6 = hop(s2, 2), hop(s4, 4), hop(s6, 6)
    got_line = hop(line_sent, 4)
    above_kept, above_sent = call(above_sum_kernel, "above_sum", ((part, F32), (part, BF16)), [whole()] * 2)(
        line_kept, got_line
    )
    got_above = hop(above_sent, 2)
    return call(
        last_kernel,
        "last",
        (((QUARTER, 3 * wide), F32),),
        [whole()] * 8,
        [pltpu.VMEM((3, QUARTER, wide), F32), pltpu.SemaphoreType.DMA((3,))],
        (pl.BlockSpec(memory_space=pltpu.HBM),),
    )(below_kept, got_below, sum_kept, r2, r4, r6, above_kept, got_above)[0]


def solution(mesh):
    in_specs = (
        P(("grp", "dev"), None, None, None),
        P(("grp", "dev"), None, None, None),
        P(("grp", "dev"), None),
        P(("grp", "dev")),
        P(("grp", "dev")),
        P(("grp", "dev"), None, None),
    )
    out_specs = P(("grp", "dev"), None)
    on_device = on_square if mesh.shape["dev"] == 8 else on_any_slab
    return jax.shard_map(
        on_device, mesh=mesh, in_specs=in_specs, out_specs=out_specs, check_vma=False
    )
```
